32 devices in a mesh: groups: 2 (over x), seq: 16 (over z, y, core).
Axes of the slice: x: 2, y: 2, z: 4, core: 2. Of those that a mesh axis runs over, the one named last changes fastest.
Arguments:
- q_rows: bfloat16 [4096, 2048], P(('groups', 'seq')), parts along dimension 0, may hold values from -6 to 6
- k_rows: bfloat16 [4096, 2048], P(('groups', 'seq')), parts along dimension 0, may hold values from -6 to 6
- v_rows: bfloat16 [4096, 2048], P(('groups', 'seq')), parts along dimension 0, may hold values from -6 to 6
- block_of: int32 [4096, 1], P(('groups', 'seq')), parts along dimension 0, may hold values from 0 to 15; in each aligned block of 128 rows (0 to 127, 128 to 255, ...) at most 12 rows name the same one
- modality: int32 [4096], P(('groups', 'seq')), parts along dimension 0, may hold values from 0 to 2
- out_gain: float32 [3, 2048], replicated, may hold values from 0.1 to 1.9
Outputs:
- mixed: bfloat16 [4096, 2048], P(('groups', 'seq')), parts along dimension 0
The draws below stay inside these ranges and needn't reach their ends.
There are 2 independent parts, one for each index of `groups`. The reference program is written for one: setup_inputs(seed, part) draws one part's arguments, and reference() takes and returns one part's arrays. A program takes and returns all parts, laid end to end along the dimension named above; an argument that names none is the same for every part. Nothing has to cross between parts.
Inputs may be any that keep to these rules, and one draw needn't show every extreme that they name: `block_of`: among the rows of one device no block is named more than 12 times, and some block is named exactly 12 times by the rows of some device.
All inputs are finite; a program needn't handle non-finite values.
Results may differ from the reference program's by a relative error of at most 0.0057.
Values may be sent and summed in bfloat16 or wider, within the bound.
A program may use at most 192 MiB of HBM per device.

```python
import math
import jax
import jax.numpy as jnp
import numpy as np
from jax import lax

HEADS = 16
HEAD_DIM = 128
MODES = 3
TOK_DEV = 128
CAP = 12
TOKENS = 2048
N_SEQ = 16


def plant(entries, stream_key, least, high):
    shape = entries.shape
    place = [jax.random.randint(jax.random.fold_in(stream_key, axis), (), 0, shape[axis]) for axis in range(len(shape))]
    entries = entries.at[tuple(place)].set(least)
    longest = shape.index(max(shape))
    place[longest] = (place[longest] + 1) % shape[longest]
    return entries.at[tuple(place)].set(high)


def block_scale(stream_key, extent, shards, smallest, largest):
    level, own = 1.0, jax.random.fold_in(stream_key, 6)
    for axis_at, blocks in shards:
        draws = jnp.exp(jax.random.uniform(jax.random.fold_in(own, axis_at), (blocks,), jnp.float32, smallest / len(shards), largest / len(shards)))
        level = level * jnp.repeat(draws, extent[axis_at] // blocks).reshape([-1 if axis == axis_at else 1 for axis in range(len(extent))])
    return level


def routed_block(own_key, own, number, rows, number_of, top, reach, slope):
    sequence = jax.random.permutation(own_key, number_of)
    crowded, ordinary = portions_of(number_of, rows * top, reach, slope, True), portions_of(number_of, rows * top, reach, slope, False)
    places = jnp.arange(number_of)

    def named(lengths, turn):
        used = int((lengths > 0).sum())
        fixed = max(1, used // 4)
        moved = fixed + (places - fixed + turn * (used - fixed)) % max(1, number_of - fixed)
        return jnp.zeros((number_of,), jnp.int32).at[sequence[jnp.where(places < fixed, places, moved)]].set(jnp.asarray(lengths, jnp.int32))

    lengths = jnp.where(number % 4 == 0, named(crowded, number // 4), named(ordinary, number - number // 4 - 1))
    mixed = jax.random.permutation(jax.random.fold_in(own, 3), number_of)
    source_of, taker = mixed[0:number_of // 2 * 2:2], mixed[1:number_of // 2 * 2:2]
    room = jnp.minimum(lengths[source_of] - 1, reach - lengths[taker]) // 2
    room = jnp.where((source_of == sequence[0]) | (taker == sequence[0]) | (lengths[taker] == 0), 0, jnp.maximum(room, 0))
    moved = jax.random.randint(jax.random.fold_in(own, 4), (number_of // 2,), 0, 1 << 20) % (room + 1)
    lengths = lengths.at[source_of].add(-moved).at[taker].add(moved)
    members = jnp.searchsorted(jnp.cumsum(lengths), jnp.arange(rows * top), side="right").astype(jnp.int32)
    grid = members.reshape(top, rows).T
    grid = grid[jax.random.permutation(jax.random.fold_in(own, 1), rows)]
    turn = jax.random.randint(jax.random.fold_in(own, 2), (rows, 1), 0, top)
    return jnp.take_along_axis(grid, (jnp.arange(top)[None, :] + turn) % top, axis=1)


def portions_of(count, total, reach, skew, full):
    weights = [(1 << 20) // math.isqrt(standing ** skew) + 1 for standing in range(1, count + 1)]
    largest = reach if full else min(reach, max(-(-total // count), total * weights[0] // sum(weights)))
    least = 1 if total - largest >= count - 1 else 0
    counts, rest = [largest] + [least] * (count - 1), total - largest - least * (count - 1)
    while rest > 0:
        candidates = [i for i in range(1, count) if counts[i] < largest] or [i for i in range(1, count) if counts[i] < reach]
        whole, remaining = sum([weights[i] for i in candidates]), rest
        for i in candidates:
            extra = min(reach - counts[i], max(1, remaining * weights[i] // whole), rest)
            counts[i] = counts[i] + extra
            rest = rest - extra
    return np.array(counts)


def bell_draw(rng, extent, width, reach, pieces=(), kind=jnp.bfloat16):
    level = block_scale(rng, extent, pieces, -0.22, 0.18) if pieces else 1.0
    values = jax.random.normal(rng, extent, jnp.float32) * width * level
    return jnp.minimum(jnp.maximum(values, -reach), reach).astype(kind)


def setup_inputs(seed: int = 0, part: int = 0) -> dict:
    streams_of = jax.random.split(jax.random.key(seed), 7)
    part_splits = jax.random.split(jax.random.fold_in(streams_of[6], part), 7)
    q_rows = bell_draw(part_splits[0], (TOKENS, HEADS * HEAD_DIM), 1.0, 6.0, ((0, 16),))
    k_rows = bell_draw(part_splits[1], (TOKENS, HEADS * HEAD_DIM), 1.0, 6.0, ((0, 16),))
    v_rows = bell_draw(part_splits[2], (TOKENS, HEADS * HEAD_DIM), 1.0, 6.0, ((0, 16),))
    block_of_keys = jax.random.split(jax.random.fold_in(part_splits[3], 1), TOKENS // TOK_DEV)
    block_of_turns = jax.random.permutation(jax.random.fold_in(part_splits[3], 3), TOKENS // TOK_DEV)
    block_of = jax.vmap(lambda own, number: routed_block(jax.random.fold_in(part_splits[3], 2), own, number, TOK_DEV, N_SEQ, 1, CAP, 1))(block_of_keys, block_of_turns).reshape((TOKENS, 1))
    modality = plant(jax.random.randint(part_splits[4], (TOKENS,), 0, 3), jax.random.fold_in(part_splits[4], 1), 0, 2).astype(jnp.int32)
    out_gain = jnp.clip(1.0 + 0.18 * jax.random.normal(streams_of[5], (MODES, HEADS * HEAD_DIM), jnp.float32), 0.1, 1.9)
    return dict(q_rows=q_rows, k_rows=k_rows, v_rows=v_rows, block_of=block_of, modality=modality, out_gain=out_gain)


def reference(q_rows, k_rows, v_rows, block_of, modality, out_gain):
    row_total = q_rows.shape[0]
    row_width = q_rows.shape[1]
    slot_count = N_SEQ * CAP
    target = block_of[:, 0].astype(jnp.int32)
    member = (target[:, None] == jnp.arange(N_SEQ, dtype=jnp.int32)[None, :]).astype(jnp.int32)
    slot_rank = lax.optimization_barrier(jnp.sum((jnp.cumsum(member, axis=0) - 1) * member, axis=1)).astype(jnp.int32)
    flat_slot = (target * slot_count + slot_rank).astype(jnp.int32)
    table = jnp.full((N_SEQ * slot_count,), row_total, jnp.int32)
    table = table.at[flat_slot].set(jnp.arange(row_total, dtype=jnp.int32)).reshape(N_SEQ, slot_count)
    padding = jnp.zeros((1, row_width), q_rows.dtype)
    q_padded = jnp.concatenate([q_rows, padding], axis=0)
    k_padded = jnp.concatenate([k_rows, padding], axis=0)
    v_padded = jnp.concatenate([v_rows, padding], axis=0)
    causal = jnp.arange(slot_count)[:, None] >= jnp.arange(slot_count)[None, :]

    def advance(prefix, row_ids):
        shape_three = (slot_count, HEADS, HEAD_DIM)
        queries = q_padded[row_ids].reshape(shape_three).astype(jnp.float32)
        key_rows = k_padded[row_ids].reshape(shape_three).astype(jnp.float32)
        value_rows = v_padded[row_ids].reshape(shape_three).astype(jnp.float32)
        block_sum = jnp.einsum('shd,she->hde', key_rows, value_rows)
        rounded = lax.optimization_barrier(prefix.astype(jnp.bfloat16)).astype(jnp.float32)
        carried_part = jnp.einsum('shd,hde->she', queries, rounded)
        scores = jnp.einsum('thd,shd->hts', queries, key_rows)
        weights = lax.optimization_barrier(jnp.where(causal[None], scores, 0.0).astype(jnp.bfloat16)).astype(jnp.float32)
        local_part = jnp.einsum('hts,she->the', weights, value_rows)
        combined = carried_part + local_part
        scale = lax.rsqrt(lax.optimization_barrier(jnp.mean(combined * combined, axis=-1, keepdims=True)) + 1e-06)
        normed = (combined * scale).astype(jnp.bfloat16)
        return (prefix + block_sum, normed.reshape(slot_count, row_width))
    start = jnp.zeros((HEADS, HEAD_DIM, HEAD_DIM), jnp.float32)
    final_prefix, outputs = lax.scan(advance, start, table)
    returned = outputs.reshape(N_SEQ * slot_count, row_width)[flat_slot]
    gains = out_gain[modality]
    return (returned.astype(jnp.float32) * gains).astype(jnp.bfloat16)
```

```python
import functools
import math

import jax
import jax.numpy as jnp
from jax import lax
from jax.experimental import pallas as pl
from jax.experimental.pallas import tpu as pltpu
from jax.sharding import PartitionSpec as P

HEADS = 16
HEAD_DIM = 128
QUERY_TILE = 256


def partner(place, distance, count):
    total, bit = 0, 1
    while bit < count:
        total = total + lax.rem(lax.div(place, bit) + lax.div(distance, bit), 2) * bit
        bit *= 2
    return total


def heads_kernel(
    count, q_ref, k_ref, v_ref, key_ref, out_ref,
    q_all, k_all, v_all, key_all, key_col, total, result,
    send_sem, recv_sem, local_sem,
):
    rows = q_ref.shape[0]
    width = q_all.shape[1]
    me = lax.axis_index("seq")

    def at_rows(place):
        return pl.ds(pl.multiple_of(place * rows, rows), rows)

    def at_columns(place):
        return pl.ds(pl.multiple_of(place * width, width), width)

    def outgoing(kind, distance):
        other = partner(me, distance, count)
        if kind == 3:
            source, target = key_ref, key_all.at[me]
        elif kind == 4:
            source, target = result.at[at_rows(other)], out_ref.at[:, at_columns(me)]
        else:
            source = (q_ref, k_ref, v_ref)[kind].at[:, at_columns(other)]
            target = (q_all, k_all, v_all)[kind].at[at_rows(me)]
        return pltpu.make_async_remote_copy(
            src_ref=source, dst_ref=target,
            send_sem=send_sem.at[kind, distance], recv_sem=recv_sem.at[kind, distance],
            device_id={"seq": other}, device_id_type=pl.DeviceIdType.MESH,
        )

    def incoming(kind, distance):
        other = partner(me, distance, count)
        if kind == 3:
            source, target = key_ref, key_all.at[other]
        elif kind == 4:
            source, target = result.at[at_rows(other)], out_ref.at[:, at_columns(other)]
        else:
            source = (q_ref, k_ref, v_ref)[kind].at[:, at_columns(other)]
            target = (q_all, k_all, v_all)[kind].at[at_rows(other)]
        return pltpu.make_async_remote_copy(
            src_ref=source, dst_ref=target,
            send_sem=send_sem.at[kind, distance], recv_sem=recv_sem.at[kind, distance],
            device_id={"seq": other}, device_id_type=pl.DeviceIdType.MESH,
        )

    barrier = pltpu.get_barrier_semaphore()

    def greet(step, _):
        pl.semaphore_signal(
            barrier, inc=1, device_id={"seq": partner(me, step + 1, count)},
            device_id_type=pl.DeviceIdType.MESH,
        )
        return 0

    lax.fori_loop(0, count - 1, greet, 0)

    own = [
        pltpu.make_async_copy(src.at[:, at_columns(me)], dst.at[at_rows(me)], local_sem.at[kind])
        for kind, (src, dst) in enumerate(((q_ref, q_all), (k_ref, k_all), (v_ref, v_all)))
    ] + [pltpu.make_async_copy(key_ref, key_all.at[me], local_sem.at[3])]
    for copy in own:
        copy.start()
    total[...] = jnp.zeros_like(total)
    pl.semaphore_wait(barrier, count - 1)

    def send_first(step, _):
        outgoing(3, count - 1 - step).start()
        outgoing(0, count - 1 - step).start()
        return 0

    def send_second(step, _):
        outgoing(1, count - 1 - step).start()
        outgoing(2, count - 1 - step).start()
        return 0

    lax.fori_loop(0, count - 1, send_first, 0)
    lax.fori_loop(0, count - 1, send_second, 0)
    for copy in own:
        copy.wait()

    def place_keys(place):
        line = jnp.broadcast_to(key_all[place][0:1], (rows, rows))
        key_col[at_rows(place), :] = line.T

    place_keys(me)

    def arrive(step, _):
        distance = count - 1 - step
        incoming(3, distance).wait_recv()
        place_keys(partner(me, distance, count))
        incoming(0, distance).wait_recv()
        return 0

    lax.fori_loop(0, count - 1, arrive, 0)

    tokens = q_all.shape[0]
    tile = math.gcd(tokens, QUERY_TILE)

    def attend(place):
        line = key_all[place][0:1]
        for head in range(width // HEAD_DIM):
            lanes = slice(head * HEAD_DIM, (head + 1) * HEAD_DIM)
            keys = k_all[at_rows(place), lanes]
            values = v_all[at_rows(place), lanes]
            for start in range(0, tokens, tile):
                part = slice(start, start + tile)
                scores = lax.dot_general(
                    q_all[part, lanes], keys, (((1,), (1,)), ((), ())),
                    preferred_element_type=jnp.float32,
                )
                weights = jnp.where(key_col[part, :] >= line, scores, 0.0).astype(jnp.bfloat16)
                total[part, lanes] += jnp.dot(weights, values, preferred_element_type=jnp.float32)

    def one_source(step, _):
        distance = count - step

        @pl.when(step > 0)
        def _():
            incoming(1, distance).wait_recv()
            incoming(2, distance).wait_recv()

        attend(partner(me, lax.rem(distance, count), count))
        return 0

    lax.fori_loop(0, count, one_source, 0)

    def finish(place):
        for head in range(width // HEAD_DIM):
            lanes = slice(head * HEAD_DIM, (head + 1) * HEAD_DIM)
            combined = total[at_rows(place), lanes]
            scale = lax.rsqrt(jnp.mean(combined * combined, axis=-1, keepdims=True) + 1e-06)
            result[at_rows(place), lanes] = (combined * scale).astype(jnp.bfloat16)

    def give_back(step, _):
        distance = count - 1 - step
        finish(partner(me, distance, count))
        outgoing(4, distance).start()
        return 0

    lax.fori_loop(0, count - 1, give_back, 0)
    finish(me)
    last = pltpu.make_async_copy(result.at[at_rows(me)], out_ref.at[:, at_columns(me)], local_sem.at[0])
    last.start()
    last.wait()

    def settle(step, _):
        distance = count - 1 - step
        for kind in range(5):
            outgoing(kind, distance).wait_send()
        incoming(4, distance).wait_recv()
        return 0

    lax.fori_loop(0, count - 1, settle, 0)


def attend_by_heads(q_rows, k_rows, v_rows, block_of):
    rows, row_width = q_rows.shape
    count = lax.axis_size("seq")
    tokens = rows * count
    width = row_width // count
    place = lax.axis_index("seq") * rows + jnp.arange(rows, dtype=jnp.int32)
    key = (block_of[:, 0] * tokens + place).astype(jnp.float32)
    key = jnp.broadcast_to(key[None, :], (8, rows))
    vmem = pl.BlockSpec(memory_space=pltpu.VMEM)
    shared = pltpu.VMEM((tokens, width), q_rows.dtype)
    return pl.pallas_call(
        functools.partial(heads_kernel, count),
        out_shape=jax.ShapeDtypeStruct((rows, row_width), q_rows.dtype),
        in_specs=[vmem] * 4,
        out_specs=vmem,
        scratch_shapes=[
            shared, shared, shared,
            pltpu.VMEM((count, 8, rows), jnp.float32),
            pltpu.VMEM((tokens, rows), jnp.float32),
            pltpu.VMEM((tokens, width), jnp.float32),
            shared,
            pltpu.SemaphoreType.DMA((5, count)),
            pltpu.SemaphoreType.DMA((5, count)),
            pltpu.SemaphoreType.DMA((4,)),
        ],
        compiler_params=pltpu.CompilerParams(
            collective_id=0, has_side_effects=True, vmem_limit_bytes=40 * 2**20
        ),
        cost_estimate=pl.CostEstimate(
            flops=4 * tokens * tokens * width, bytes_accessed=8 * rows * row_width, transcendentals=tokens
        ),
    )(q_rows, k_rows, v_rows, key)


def entering(part, axis):
    place = lax.axis_index(axis)
    count = lax.axis_size(axis)
    state = lax.ppermute(part, axis, [(i, i + 1) for i in range(count - 1)])
    reach = 1
    while reach < count:
        state = state + lax.ppermute(state, axis, [(i, i + reach) for i in range(count - reach)])
        reach *= 2
    return state


def block_state(key_rows, value_rows):
    return jnp.einsum("shd,she->hde", key_rows, value_rows, preferred_element_type=jnp.float32)


def attend(queries, row_order, key_rows, value_rows, carried):
    row_count = queries.shape[0]
    head_count = queries.shape[1]
    slot_count = key_rows.shape[0]
    group_size = math.gcd(head_count, 4)
    carried_part = jnp.einsum("rhd,hde->rhe", queries, carried, preferred_element_type=jnp.float32)
    causal = row_order[:, None] >= jnp.arange(slot_count, dtype=jnp.int32)[None, :]

    def one_group(group_id):
        query_group = lax.dynamic_slice_in_dim(queries, group_id * group_size, group_size, 1)
        key_group = lax.dynamic_slice_in_dim(key_rows, group_id * group_size, group_size, 1)
        value_group = lax.dynamic_slice_in_dim(value_rows, group_id * group_size, group_size, 1)
        scores = jnp.einsum(
            "rhd,shd->hrs", query_group, key_group, preferred_element_type=jnp.float32
        )
        weights = jnp.where(causal[None], scores, 0.0).astype(jnp.bfloat16)
        return jnp.einsum("hrs,she->rhe", weights, value_group, preferred_element_type=jnp.float32)

    pieces = lax.map(one_group, jnp.arange(head_count // group_size, dtype=jnp.int32))
    local_part = jnp.moveaxis(pieces, 0, 1).reshape(row_count, head_count, queries.shape[2])
    combined = carried_part + local_part
    scale = lax.rsqrt(jnp.mean(combined * combined, axis=-1, keepdims=True) + 1e-06)
    return (combined * scale).astype(jnp.bfloat16)


def attend_by_blocks(q_rows, k_rows, v_rows, block_of):
    tok_count = q_rows.shape[0]
    row_width = q_rows.shape[1]
    peer_count = lax.axis_size("seq")
    capacity = max(2, 3 * tok_count // (2 * peer_count))
    slot_count = peer_count * capacity
    target = block_of[:, 0]
    place = jnp.arange(tok_count, dtype=jnp.int32)
    earlier_same = (target[:, None] == target[None, :]) & (place[None, :] < place[:, None])
    slot_rank = jnp.sum(earlier_same.astype(jnp.int32), axis=1)
    slot_index = target * capacity + slot_rank

    def routed(row_block):
        buffer = jnp.zeros((slot_count, row_width), row_block.dtype).at[slot_index].set(row_block)
        moved = lax.all_to_all(
            buffer.reshape(peer_count, capacity, row_width), "seq", split_axis=0, concat_axis=0, tiled=True
        )
        return moved.reshape(slot_count, HEADS, HEAD_DIM)

    queries, key_rows, value_rows = routed(q_rows), routed(k_rows), routed(v_rows)
    prefix = entering(block_state(key_rows, value_rows), "seq")
    carried = prefix.astype(jnp.bfloat16)
    normed = attend(queries, jnp.arange(slot_count, dtype=jnp.int32), key_rows, value_rows, carried)
    returned = lax.all_to_all(
        normed.reshape(peer_count, capacity, row_width), "seq", split_axis=0, concat_axis=0, tiled=True
    )
    return returned.reshape(slot_count, row_width)[slot_index]


def on_device(q_rows, k_rows, v_rows, block_of, modality, out_gain):
    count = lax.axis_size("seq")
    plan = attend_by_heads if count > 1 and HEADS % count == 0 else attend_by_blocks
    own_rows = plan(q_rows, k_rows, v_rows, block_of)
    chosen = modality[:, None]
    gains = jnp.where(
        chosen == 0,
        out_gain[0][None, :],
        jnp.where(chosen == 1, out_gain[1][None, :], out_gain[2][None, :]),
    )
    return (own_rows.astype(jnp.float32) * gains).astype(jnp.bfloat16)


def solution(mesh):
    placed = (
        P(("groups", "seq"), None),
        P(("groups", "seq"), None),
        P(("groups", "seq"), None),
        P(("groups", "seq"), None),
        P(("groups", "seq")),
        P(),
    )
    return jax.shard_map(
        on_device, mesh=mesh, in_specs=placed, out_specs=P(("groups", "seq"), None), check_vma=False
    )
```

```python
import functools
import math

import jax
import jax.numpy as jnp
from jax import lax
from jax.experimental import pallas as pl
from jax.experimental.pallas import tpu as pltpu
from jax.sharding import PartitionSpec as P

HEADS = 16
HEAD_DIM = 128
BLOCK_ROWS = 16


def partner(place, distance, count):
    total, bit = 0, 1
    while bit < count:
        total = total + lax.rem(lax.div(place, bit) + lax.div(distance, bit), 2) * bit
        bit *= 2
    return total


def heads_kernel(
    count, q_hbm, k_hbm, v_hbm, block_hbm, out_ref,
    raw, raw_block, outbox, inbox, key_line, key_col, total, result,
    send_sem, recv_sem, local_sem,
):
    rows = raw.shape[1]
    width = inbox.shape[2]
    first = rows + BLOCK_ROWS
    tokens = total.shape[0]
    pairs = count // 2
    me = lax.axis_index("seq")
    parts = (slice(0, first), slice(first, first + 2 * rows))

    def at_rows(place, size):
        return pl.ds(pl.multiple_of(place * size, size), size)

    def across(kind, distance, sending):
        other = partner(me, distance, count)
        at, at_out = (me, me) if sending else (other, other)
        if kind == 2:
            source, target = result.at[at_rows(other, rows)], out_ref.at[:, at_rows(at_out, width)]
        else:
            source, target = outbox.at[other, parts[kind]], inbox.at[at, parts[kind]]
        return pltpu.make_async_remote_copy(
            src_ref=source, dst_ref=target,
            send_sem=send_sem.at[kind, distance], recv_sem=recv_sem.at[kind, distance],
            device_id={"seq": other}, device_id_type=pl.DeviceIdType.MESH,
        )

    load = [
        pltpu.make_async_copy(src, raw.at[kind], local_sem.at[kind])
        for kind, src in enumerate((q_hbm, k_hbm, v_hbm))
    ]
    load_block = pltpu.make_async_copy(block_hbm, raw_block, local_sem.at[3])
    load_block.start()
    for copy in load:
        copy.start()

    barrier = pltpu.get_barrier_semaphore()

    def greet(step, _):
        pl.semaphore_signal(
            barrier, inc=1, device_id={"seq": partner(me, step + 1, count)},
            device_id_type=pl.DeviceIdType.MESH,
        )
        return 0

    lax.fori_loop(0, count - 1, greet, 0)

    def sort_out(kind, start):
        load[kind].wait()
        for other in range(count):
            outbox[other, start:start + rows, :] = raw[kind, :, other * width:(other + 1) * width]

    def far_first(step):
        return lax.rem(count - step, count)

    load_block.wait()
    blocks = jnp.broadcast_to(raw_block[...].astype(jnp.float32), (BLOCK_ROWS, rows)).astype(outbox.dtype)
    for other in range(count):
        outbox[other, rows:first, 0:rows] = blocks
    sort_out(0, 0)
    pl.semaphore_wait(barrier, count - 1)

    def send(kind):
        def one(step, _):
            across(kind, far_first(step + 1), True).start()
            return 0

        lax.fori_loop(0, count - 1, one, 0)

    send(0)
    sort_out(1, first)
    sort_out(2, first + rows)
    send(1)
    own = pltpu.make_async_copy(outbox.at[me], inbox.at[me], local_sem.at[3])
    own.start()
    total[...] = jnp.zeros_like(total)
    own.wait()

    def place_keys(place):
        block = inbox[place, rows:first, 0:rows][0:1].astype(jnp.float32)
        row = lax.broadcasted_iota(jnp.int32, (1, rows), 1) + place * rows
        line = block * tokens + row.astype(jnp.float32)
        key_line[:, at_rows(place, rows)] = jnp.broadcast_to(line, (8, rows))
        key_col[at_rows(place, rows), :] = jnp.broadcast_to(line, (rows, rows)).T

    place_keys(me)

    def arrive(step, _):
        distance = far_first(step + 1)
        across(0, distance, False).wait_recv()
        place_keys(partner(me, distance, count))
        return 0

    lax.fori_loop(0, count - 1, arrive, 0)

    def both(pair, start, lanes):
        return inbox[pl.ds(2 * pair, 2), start:start + rows, lanes].reshape(2 * rows, HEAD_DIM)

    def attended(query_pair, key_pair, lanes):
        scores = lax.dot_general(
            both(query_pair, 0, lanes), both(key_pair, first, lanes), (((1,), (1,)), ((), ())),
            preferred_element_type=jnp.float32,
        )
        column = key_col[at_rows(query_pair, 2 * rows), :]
        line = key_line[0:1, at_rows(key_pair, 2 * rows)]
        causal = jnp.concatenate([column >= line[:, :rows], column >= line[:, rows:]], axis=1)
        weights = jnp.where(causal, scores, 0.0).astype(jnp.bfloat16)
        return jnp.dot(weights, both(key_pair, first + rows, lanes), preferred_element_type=jnp.float32)

    shares = [slice(start, start + HEAD_DIM) for start in range(0, width, HEAD_DIM)]

    def wait_pair(distance):
        across(1, 2 * distance + 1, False).wait_recv()

        @pl.when(distance > 0)
        def _():
            across(1, 2 * distance, False).wait_recv()

    def one_pair(step, _):
        distance = lax.rem(pairs - step, pairs)
        wait_pair(distance)
        key_pair = partner(lax.div(me, 2), distance, pairs)
        for lanes in shares:
            for query_pair in range(pairs):
                total[query_pair * 2 * rows:(query_pair + 1) * 2 * rows, lanes] += attended(
                    query_pair, key_pair, lanes
                )
        return 0

    lax.fori_loop(1, pairs, one_pair, 0)
    wait_pair(0)

    def finish(step, _):
        distance = lax.rem(2 * pairs - 1 - step, pairs)
        query_pair = partner(lax.div(me, 2), distance, pairs)
        at = at_rows(query_pair, 2 * rows)
        for lanes in shares:
            combined = total[at, lanes] + attended(query_pair, lax.div(me, 2), lanes)
            scale = lax.rsqrt(jnp.mean(combined * combined, axis=-1, keepdims=True) + 1e-06)
            result[at, lanes] = (combined * scale).astype(jnp.bfloat16)
        across(2, 2 * distance + 1, True).start()

        @pl.when(distance > 0)
        def _():
            across(2, 2 * distance, True).start()

        return 0

    lax.fori_loop(0, pairs, finish, 0)
    last = pltpu.make_async_copy(
        result.at[at_rows(me, rows)], out_ref.at[:, at_rows(me, width)], local_sem.at[3]
    )
    last.start()
    last.wait()

    def settle(step, _):
        distance = far_first(step + 1)
        for kind in range(3):
            across(kind, distance, True).wait_send()
        across(2, distance, False).wait_recv()
        return 0

    lax.fori_loop(0, count - 1, settle, 0)


def attend_by_heads(q_rows, k_rows, v_rows, block_of):
    rows, row_width = q_rows.shape
    count = lax.axis_size("seq")
    tokens = rows * count
    width = row_width // count
    anywhere = pl.BlockSpec(memory_space=pl.ANY)
    message = pltpu.VMEM((count, 3 * rows + BLOCK_ROWS, width), q_rows.dtype)
    return pl.pallas_call(
        functools.partial(heads_kernel, count),
        out_shape=jax.ShapeDtypeStruct((rows, row_width), q_rows.dtype),
        in_specs=[anywhere] * 4,
        out_specs=pl.BlockSpec(memory_space=pltpu.VMEM),
        scratch_shapes=[
            pltpu.VMEM((3, rows, row_width), q_rows.dtype),
            pltpu.VMEM((1, rows), jnp.int32),
            message,
            message,
            pltpu.VMEM((8, tokens), jnp.float32),
            pltpu.VMEM((tokens, rows), jnp.float32),
            pltpu.VMEM((tokens, width), jnp.float32),
            pltpu.VMEM((tokens, width), q_rows.dtype),
            pltpu.SemaphoreType.DMA((3, count)),
            pltpu.SemaphoreType.DMA((3, count)),
            pltpu.SemaphoreType.DMA((4,)),
        ],
        compiler_params=pltpu.CompilerParams(
            collective_id=0, has_side_effects=True, vmem_limit_bytes=56 * 2**20
        ),
        cost_estimate=pl.CostEstimate(
            flops=4 * tokens * tokens * width, bytes_accessed=8 * rows * row_width, transcendentals=tokens
        ),
    )(q_rows, k_rows, v_rows, block_of.reshape(1, rows))


def entering(part, axis):
    place = lax.axis_index(axis)
    count = lax.axis_size(axis)
    state = lax.ppermute(part, axis, [(i, i + 1) for i in range(count - 1)])
    reach = 1
    while reach < count:
        state = state + lax.ppermute(state, axis, [(i, i + reach) for i in range(count - reach)])
        reach *= 2
    return state


def block_state(key_rows, value_rows):
    return jnp.einsum("shd,she->hde", key_rows, value_rows, preferred_element_type=jnp.float32)


def attend(queries, row_order, key_rows, value_rows, carried):
    row_count = queries.shape[0]
    head_count = queries.shape[1]
    slot_count = key_rows.shape[0]
    group_size = math.gcd(head_count, 4)
    carried_part = jnp.einsum("rhd,hde->rhe", queries, carried, preferred_element_type=jnp.float32)
    causal = row_order[:, None] >= jnp.arange(slot_count, dtype=jnp.int32)[None, :]

    def one_group(group_id):
        query_group = lax.dynamic_slice_in_dim(queries, group_id * group_size, group_size, 1)
        key_group = lax.dynamic_slice_in_dim(key_rows, group_id * group_size, group_size, 1)
        value_group = lax.dynamic_slice_in_dim(value_rows, group_id * group_size, group_size, 1)
        scores = jnp.einsum(
            "rhd,shd->hrs", query_group, key_group, preferred_element_type=jnp.float32
        )
        weights = jnp.where(causal[None], scores, 0.0).astype(jnp.bfloat16)
        return jnp.einsum("hrs,she->rhe", weights, value_group, preferred_element_type=jnp.float32)

    pieces = lax.map(one_group, jnp.arange(head_count // group_size, dtype=jnp.int32))
    local_part = jnp.moveaxis(pieces, 0, 1).reshape(row_count, head_count, queries.shape[2])
    combined = carried_part + local_part
    scale = lax.rsqrt(jnp.mean(combined * combined, axis=-1, keepdims=True) + 1e-06)
    return (combined * scale).astype(jnp.bfloat16)


def attend_by_blocks(q_rows, k_rows, v_rows, block_of):
    tok_count = q_rows.shape[0]
    row_width = q_rows.shape[1]
    peer_count = lax.axis_size("seq")
    capacity = max(2, 3 * tok_count // (2 * peer_count))
    slot_count = peer_count * capacity
    target = block_of[:, 0]
    place = jnp.arange(tok_count, dtype=jnp.int32)
    earlier_same = (target[:, None] == target[None, :]) & (place[None, :] < place[:, None])
    slot_rank = jnp.sum(earlier_same.astype(jnp.int32), axis=1)
    slot_index = target * capacity + slot_rank

    def routed(row_block):
        buffer = jnp.zeros((slot_count, row_width), row_block.dtype).at[slot_index].set(row_block)
        moved = lax.all_to_all(
            buffer.reshape(peer_count, capacity, row_width), "seq", split_axis=0, concat_axis=0, tiled=True
        )
        return moved.reshape(slot_count, HEADS, HEAD_DIM)

    queries, key_rows, value_rows = routed(q_rows), routed(k_rows), routed(v_rows)
    prefix = entering(block_state(key_rows, value_rows), "seq")
    carried = prefix.astype(jnp.bfloat16)
    normed = attend(queries, jnp.arange(slot_count, dtype=jnp.int32), key_rows, value_rows, carried)
    returned = lax.all_to_all(
        normed.reshape(peer_count, capacity, row_width), "seq", split_axis=0, concat_axis=0, tiled=True
    )
    return returned.reshape(slot_count, row_width)[slot_index]


def on_device(q_rows, k_rows, v_rows, block_of, modality, out_gain):
    rows = q_rows.shape[0]
    count = lax.axis_size("seq")
    by_heads = count > 1 and HEADS % count == 0 and rows == HEAD_DIM
    plan = attend_by_heads if by_heads else attend_by_blocks
    own_rows = plan(q_rows, k_rows, v_rows, block_of)
    chosen = modality[:, None]
    gains = jnp.where(
        chosen == 0,
        out_gain[0][None, :],
        jnp.where(chosen == 1, out_gain[1][None, :], out_gain[2][None, :]),
    )
    return (own_rows.astype(jnp.float32) * gains).astype(jnp.bfloat16)


def solution(mesh):
    placed = (
        P(("groups", "seq"), None),
        P(("groups", "seq"), None),
        P(("groups", "seq"), None),
        P(("groups", "seq"), None),
        P(("groups", "seq")),
        P(),
    )
    return jax.shard_map(
        on_device, mesh=mesh, in_specs=placed, out_specs=P(("groups", "seq"), None), check_vma=False
    )
```

```python
import functools
import math

import jax
import jax.numpy as jnp
from jax import lax
from jax.experimental import pallas as pl
from jax.experimental.pallas import tpu as pltpu
from jax.sharding import PartitionSpec as P

HEADS = 16
HEAD_DIM = 128
BLOCK_ROWS = 16
FAR_WINDOW = 2


def partner(place, distance, count):
    total, bit = 0, 1
    while bit < count:
        total = total + lax.rem(lax.div(place, bit) + lax.div(distance, bit), 2) * bit
        bit *= 2
    return total


def heads_kernel(
    count, q_hbm, k_hbm, v_hbm, block_hbm, mode_hbm, gain_hbm, out_ref,
    raw, raw_block, raw_mode, gains, outbox, inbox, key_line, key_col, mode_col, total, result, back,
    send_sem, recv_sem, local_sem,
):
    rows = raw.shape[1]
    width = inbox.shape[2]
    first = rows + BLOCK_ROWS
    tokens = total.shape[0]
    pairs = count // 2
    me = lax.axis_index("seq")
    parts = (slice(0, first), slice(first, first + 2 * rows))

    def at_rows(place, size):
        return pl.ds(pl.multiple_of(place * size, size), size)

    def across(kind, distance, sending):
        other = partner(me, distance, count)
        at = me if sending else other
        if kind == 2:
            source, target = result.at[at_rows(other, rows)], back.at[at]
        else:
            source, target = outbox.at[other, parts[kind]], inbox.at[at, parts[kind]]
        return pltpu.make_async_remote_copy(
            src_ref=source, dst_ref=target,
            send_sem=send_sem.at[kind, distance], recv_sem=recv_sem.at[kind, distance],
            device_id={"seq": other}, device_id_type=pl.DeviceIdType.MESH,
        )

    load = [
        pltpu.make_async_copy(src, raw.at[kind], local_sem.at[kind])
        for kind, src in enumerate((q_hbm, k_hbm, v_hbm))
    ]
    load_block = pltpu.make_async_copy(block_hbm, raw_block, local_sem.at[3])
    load_mode = pltpu.make_async_copy(mode_hbm, raw_mode, local_sem.at[4])
    load_gain = pltpu.make_async_copy(gain_hbm, gains, local_sem.at[5])
    for copy in (load_block, *load, load_mode, load_gain):
        copy.start()

    barrier = pltpu.get_barrier_semaphore()

    def greet(step, _):
        pl.semaphore_signal(
            barrier, inc=1, device_id={"seq": partner(me, step + 1, count)},
            device_id_type=pl.DeviceIdType.MESH,
        )
        return 0

    lax.fori_loop(0, count - 1, greet, 0)

    def sort_out(kind, start):
        load[kind].wait()
        for other in range(count):
            outbox[other, start:start + rows, :] = raw[kind, :, other * width:(other + 1) * width]

    def far_first(step):
        return lax.rem(count - step, count)

    load_block.wait()
    blocks = jnp.broadcast_to(raw_block[...].astype(jnp.float32), (BLOCK_ROWS, rows)).astype(outbox.dtype)
    for other in range(count):
        outbox[other, rows:first, 0:rows] = blocks
    sort_out(0, 0)
    pl.semaphore_wait(barrier, count - 1)

    near = pairs // 2
    far = pairs - near
    window = min(FAR_WINDOW, far)

    def send_first(step, _):
        across(0, far_first(step + 1), True).start()
        return 0

    def send_pair(distance):
        across(1, 2 * distance + 1, True).start()

        @pl.when(distance > 0)
        def _():
            across(1, 2 * distance, True).start()

    def send_near(distance, _):
        send_pair(distance)
        return 0

    def send_far(step, _):
        send_pair(pairs - 1 - step)
        return 0

    lax.fori_loop(0, count - 1, send_first, 0)
    sort_out(1, first)
    sort_out(2, first + rows)
    lax.fori_loop(0, window, send_far, 0)
    lax.fori_loop(0, near, send_near, 0)
    own = pltpu.make_async_copy(outbox.at[me], inbox.at[me], local_sem.at[3])
    own.start()
    total[...] = jnp.zeros_like(total)
    load_mode.wait()
    load_gain.wait()
    mode_col[...] = jnp.broadcast_to(raw_mode[...].astype(jnp.float32), (rows, rows)).T
    own.wait()

    def place_keys(place):
        block = inbox[place, rows:first, 0:rows][0:1].astype(jnp.float32)
        row = lax.broadcasted_iota(jnp.int32, (1, rows), 1) + place * rows
        line = block * tokens + row.astype(jnp.float32)
        key_line[:, at_rows(place, rows)] = jnp.broadcast_to(line, (8, rows))
        key_col[at_rows(place, rows), :] = jnp.broadcast_to(line, (rows, rows)).T

    place_keys(me)

    def arrive(step, _):
        distance = far_first(step + 1)
        across(0, distance, False).wait_recv()
        place_keys(partner(me, distance, count))
        return 0

    lax.fori_loop(0, count - 1, arrive, 0)

    def both(pair, start, lanes):
        return inbox[pl.ds(2 * pair, 2), start:start + rows, lanes].reshape(2 * rows, HEAD_DIM)

    def attended(query_pair, key_pair, lanes):
        scores = lax.dot_general(
            both(query_pair, 0, lanes), both(key_pair, first, lanes), (((1,), (1,)), ((), ())),
            preferred_element_type=jnp.float32,
        )
        column = key_col[at_rows(query_pair, 2 * rows), :]
        line = key_line[0:1, at_rows(key_pair, 2 * rows)]
        causal = jnp.concatenate([column >= line[:, :rows], column >= line[:, rows:]], axis=1)
        weights = jnp.where(causal, scores, 0.0).astype(jnp.bfloat16)
        return jnp.dot(weights, both(key_pair, first + rows, lanes), preferred_element_type=jnp.float32)

    shares = [slice(start, start + HEAD_DIM) for start in range(0, width, HEAD_DIM)]

    def wait_pair(distance):
        across(1, 2 * distance + 1, False).wait_recv()

        @pl.when(distance > 0)
        def _():
            across(1, 2 * distance, False).wait_recv()

    def take_keys(distance):
        key_pair = partner(lax.div(me, 2), distance, pairs)
        for lanes in shares:
            for query_pair in range(pairs):
                total[query_pair * 2 * rows:(query_pair + 1) * 2 * rows, lanes] += attended(
                    query_pair, key_pair, lanes
                )

    def take_near(distance, _):
        wait_pair(distance)
        take_keys(distance)
        return 0

    def take_far(step, _):
        wait_pair(pairs - 1 - step)

        @pl.when(step < far - window)
        def _():
            send_pair(pairs - 1 - step - window)

        take_keys(pairs - 1 - step)
        return 0

    lax.fori_loop(0, near, take_near, 0)
    lax.fori_loop(0, far - 1, take_far, 0)
    wait_pair(near + me * 0)
    last_pair = partner(lax.div(me, 2), near, pairs)

    def finish(step, _):
        distance = pairs - 1 - step
        query_pair = partner(lax.div(me, 2), distance, pairs)
        at = at_rows(query_pair, 2 * rows)
        for lanes in shares:
            combined = total[at, lanes] + attended(query_pair, last_pair, lanes)
            scale = lax.rsqrt(jnp.mean(combined * combined, axis=-1, keepdims=True) + 1e-06)
            result[at, lanes] = (combined * scale).astype(jnp.bfloat16)
        across(2, 2 * distance + 1, True).start()

        @pl.when(distance > 0)
        def _():
            across(2, 2 * distance, True).start()

        return 0

    lax.fori_loop(0, pairs, finish, 0)

    def scaled(source, place):
        for start in range(0, width, HEAD_DIM):
            at = pl.ds(pl.multiple_of(place * width + start, HEAD_DIM), HEAD_DIM)
            gain = jnp.where(
                mode_col[...] == 0.0, gains[0:1, at],
                jnp.where(mode_col[...] == 1.0, gains[1:2, at], gains[2:3, at]),
            )
            normed = source[:, start:start + HEAD_DIM].astype(jnp.float32)
            out_ref[:, at] = (normed * gain).astype(out_ref.dtype)

    scaled(result.at[at_rows(me, rows)], me)

    def settle(step, _):
        distance = step + 1
        for kind in range(3):
            across(kind, distance, True).wait_send()
        across(2, distance, False).wait_recv()
        other = partner(me, distance, count)
        scaled(back.at[other], other)
        return 0

    lax.fori_loop(0, count - 1, settle, 0)


def attend_by_heads(q_rows, k_rows, v_rows, block_of, modality, out_gain):
    rows, row_width = q_rows.shape
    count = lax.axis_size("seq")
    tokens = rows * count
    width = row_width // count
    anywhere = pl.BlockSpec(memory_space=pl.ANY)
    message = pltpu.VMEM((count, 3 * rows + BLOCK_ROWS, width), q_rows.dtype)
    return pl.pallas_call(
        functools.partial(heads_kernel, count),
        out_shape=jax.ShapeDtypeStruct((rows, row_width), q_rows.dtype),
        in_specs=[anywhere] * 6,
        out_specs=pl.BlockSpec(memory_space=pltpu.VMEM),
        scratch_shapes=[
            pltpu.VMEM((3, rows, row_width), q_rows.dtype),
            pltpu.VMEM((1, rows), jnp.int32),
            pltpu.VMEM((1, rows), jnp.int32),
            pltpu.VMEM(out_gain.shape, jnp.float32),
            message,
            message,
            pltpu.VMEM((8, tokens), jnp.float32),
            pltpu.VMEM((tokens, rows), jnp.float32),
            pltpu.VMEM((rows, rows), jnp.float32),
            pltpu.VMEM((tokens, width), jnp.float32),
            pltpu.VMEM((tokens, width), q_rows.dtype),
            pltpu.VMEM((count, rows, width), q_rows.dtype),
            pltpu.SemaphoreType.DMA((3, count)),
            pltpu.SemaphoreType.DMA((3, count)),
            pltpu.SemaphoreType.DMA((6,)),
        ],
        compiler_params=pltpu.CompilerParams(
            collective_id=0, has_side_effects=True, vmem_limit_bytes=56 * 2**20
        ),
        cost_estimate=pl.CostEstimate(
            flops=4 * tokens * tokens * width, bytes_accessed=8 * rows * row_width, transcendentals=tokens
        ),
    )(q_rows, k_rows, v_rows, block_of.reshape(1, rows), modality.reshape(1, rows), out_gain)


def entering(part, axis):
    place = lax.axis_index(axis)
    count = lax.axis_size(axis)
    state = lax.ppermute(part, axis, [(i, i + 1) for i in range(count - 1)])
    reach = 1
    while reach < count:
        state = state + lax.ppermute(state, axis, [(i, i + reach) for i in range(count - reach)])
        reach *= 2
    return state


def block_state(key_rows, value_rows):
    return jnp.einsum("shd,she->hde", key_rows, value_rows, preferred_element_type=jnp.float32)


def attend(queries, row_order, key_rows, value_rows, carried):
    row_count = queries.shape[0]
    head_count = queries.shape[1]
    slot_count = key_rows.shape[0]
    group_size = math.gcd(head_count, 4)
    carried_part = jnp.einsum("rhd,hde->rhe", queries, carried, preferred_element_type=jnp.float32)
    causal = row_order[:, None] >= jnp.arange(slot_count, dtype=jnp.int32)[None, :]

    def one_group(group_id):
        query_group = lax.dynamic_slice_in_dim(queries, group_id * group_size, group_size, 1)
        key_group = lax.dynamic_slice_in_dim(key_rows, group_id * group_size, group_size, 1)
        value_group = lax.dynamic_slice_in_dim(value_rows, group_id * group_size, group_size, 1)
        scores = jnp.einsum(
            "rhd,shd->hrs", query_group, key_group, preferred_element_type=jnp.float32
        )
        weights = jnp.where(causal[None], scores, 0.0).astype(jnp.bfloat16)
        return jnp.einsum("hrs,she->rhe", weights, value_group, preferred_element_type=jnp.float32)

    pieces = lax.map(one_group, jnp.arange(head_count // group_size, dtype=jnp.int32))
    local_part = jnp.moveaxis(pieces, 0, 1).reshape(row_count, head_count, queries.shape[2])
    combined = carried_part + local_part
    scale = lax.rsqrt(jnp.mean(combined * combined, axis=-1, keepdims=True) + 1e-06)
    return (combined * scale).astype(jnp.bfloat16)


def attend_by_blocks(q_rows, k_rows, v_rows, block_of, modality, out_gain):
    tok_count = q_rows.shape[0]
    row_width = q_rows.shape[1]
    peer_count = lax.axis_size("seq")
    capacity = max(2, 3 * tok_count // (2 * peer_count))
    slot_count = peer_count * capacity
    target = block_of[:, 0]
    place = jnp.arange(tok_count, dtype=jnp.int32)
    earlier_same = (target[:, None] == target[None, :]) & (place[None, :] < place[:, None])
    slot_rank = jnp.sum(earlier_same.astype(jnp.int32), axis=1)
    slot_index = target * capacity + slot_rank

    def routed(row_block):
        buffer = jnp.zeros((slot_count, row_width), row_block.dtype).at[slot_index].set(row_block)
        moved = lax.all_to_all(
            buffer.reshape(peer_count, capacity, row_width), "seq", split_axis=0, concat_axis=0, tiled=True
        )
        return moved.reshape(slot_count, HEADS, HEAD_DIM)

    queries, key_rows, value_rows = routed(q_rows), routed(k_rows), routed(v_rows)
    prefix = entering(block_state(key_rows, value_rows), "seq")
    carried = prefix.astype(jnp.bfloat16)
    normed = attend(queries, jnp.arange(slot_count, dtype=jnp.int32), key_rows, value_rows, carried)
    returned = lax.all_to_all(
        normed.reshape(peer_count, capacity, row_width), "seq", split_axis=0, concat_axis=0, tiled=True
    )
    own_rows = returned.reshape(slot_count, row_width)[slot_index]
    chosen = modality[:, None]
    gains = jnp.where(
        chosen == 0,
        out_gain[0][None, :],
        jnp.where(chosen == 1, out_gain[1][None, :], out_gain[2][None, :]),
    )
    return (own_rows.astype(jnp.float32) * gains).astype(jnp.bfloat16)


def on_device(q_rows, k_rows, v_rows, block_of, modality, out_gain):
    rows = q_rows.shape[0]
    count = lax.axis_size("seq")
    by_heads = count > 1 and HEADS % count == 0 and rows == HEAD_DIM
    plan = attend_by_heads if by_heads else attend_by_blocks
    return plan(q_rows, k_rows, v_rows, block_of, modality, out_gain)


def solution(mesh):
    placed = (
        P(("groups", "seq"), None),
        P(("groups", "seq"), None),
        P(("groups", "seq"), None),
        P(("groups", "seq"), None),
        P(("groups", "seq")),
        P(),
    )
    return jax.shard_map(
        on_device, mesh=mesh, in_specs=placed, out_specs=P(("groups", "seq"), None), check_vma=False
    )
```

```python
import functools
import math

import jax
import jax.numpy as jnp
from jax import lax
from jax.experimental import pallas as pl
from jax.experimental.pallas import tpu as pltpu
from jax.sharding import PartitionSpec as P

HEADS = 16
HEAD_DIM = 128
FAR_WINDOW = 2


def partner(place, distance, count):
    total, bit = 0, 1
    while bit < count:
        total = total + lax.rem(lax.div(place, bit) + lax.div(distance, bit), 2) * bit
        bit *= 2
    return total


def heads_kernel(
    count, q_hbm, k_hbm, v_hbm, block_hbm, mode_hbm, gain_hbm, out_ref,
    raw, raw_block, raw_mode, gains, outbox, inbox, blocks, key_line, key_col, mode_col, total, result, back,
    send_sem, recv_sem, local_sem,
):
    rows = raw.shape[1]
    width = inbox.shape[2]
    first = rows
    tokens = total.shape[0]
    pairs = count // 2
    me = lax.axis_index("seq")
    parts = (slice(0, first), slice(first, first + 2 * rows))

    def at_rows(place, size):
        return pl.ds(pl.multiple_of(place * size, size), size)

    def across(kind, distance, sending):
        other = partner(me, distance, count)
        at = me if sending else other
        if kind == 2:
            source, target = result.at[at_rows(other, rows)], back.at[at]
        elif kind == 3:
            source, target = raw_block, blocks.at[at]
        else:
            source, target = outbox.at[other, parts[kind]], inbox.at[at, parts[kind]]
        return pltpu.make_async_remote_copy(
            src_ref=source, dst_ref=target,
            send_sem=send_sem.at[kind, distance], recv_sem=recv_sem.at[kind, distance],
            device_id={"seq": other}, device_id_type=pl.DeviceIdType.MESH,
        )

    load = [
        pltpu.make_async_copy(src, raw.at[kind], local_sem.at[kind])
        for kind, src in enumerate((q_hbm, k_hbm, v_hbm))
    ]
    load_block = pltpu.make_async_copy(block_hbm, raw_block, local_sem.at[3])
    load_mode = pltpu.make_async_copy(mode_hbm, raw_mode, local_sem.at[4])
    load_gain = pltpu.make_async_copy(gain_hbm, gains, local_sem.at[5])
    for copy in (load_block, *load, load_mode, load_gain):
        copy.start()

    barrier = pltpu.get_barrier_semaphore()

    def greet(step, _):
        pl.semaphore_signal(
            barrier, inc=1, device_id={"seq": partner(me, step + 1, count)},
            device_id_type=pl.DeviceIdType.MESH,
        )
        return 0

    lax.fori_loop(0, count - 1, greet, 0)

    def sort_out(kind, start):
        load[kind].wait()
        for other in range(count):
            outbox[other, start:start + rows, :] = raw[kind, :, other * width:(other + 1) * width]

    def far_first(step):
        return lax.rem(count - step, count)

    load_block.wait()
    sort_out(0, 0)
    pl.semaphore_wait(barrier, count - 1)

    near = pairs // 2
    far = pairs - near
    window = min(FAR_WINDOW, far)

    def send_first(step, _):
        across(3, far_first(step + 1), True).start()
        across(0, far_first(step + 1), True).start()
        return 0

    def send_pair(distance):
        across(1, 2 * distance + 1, True).start()

        @pl.when(distance > 0)
        def _():
            across(1, 2 * distance, True).start()

    def send_near(distance, _):
        send_pair(distance)
        return 0

    def send_far(step, _):
        send_pair(pairs - 1 - step)
        return 0

    lax.fori_loop(0, count - 1, send_first, 0)
    sort_out(1, first)
    sort_out(2, first + rows)
    lax.fori_loop(0, window, send_far, 0)
    lax.fori_loop(0, near, send_near, 0)
    own = pltpu.make_async_copy(outbox.at[me], inbox.at[me], local_sem.at[3])
    own.start()
    blocks[me] = raw_block[...]
    total[...] = jnp.zeros_like(total)
    load_mode.wait()
    load_gain.wait()
    mode_col[...] = jnp.broadcast_to(raw_mode[...].astype(jnp.float32), (rows, rows)).T
    own.wait()

    def place_keys(place):
        block = blocks[place].astype(jnp.float32)
        row = lax.broadcasted_iota(jnp.int32, (1, rows), 1) + place * rows
        line = block * tokens + row.astype(jnp.float32)
        key_line[:, at_rows(place, rows)] = jnp.broadcast_to(line, (8, rows))
        key_col[at_rows(place, rows), :] = jnp.broadcast_to(line, (rows, rows)).T

    place_keys(me)

    def arrive(step, _):
        distance = far_first(step + 1)
        across(3, distance, False).wait_recv()
        across(0, distance, False).wait_recv()
        place_keys(partner(me, distance, count))
        return 0

    lax.fori_loop(0, count - 1, arrive, 0)

    def both(pair, start, lanes):
        return inbox[pl.ds(2 * pair, 2), start:start + rows, lanes].reshape(2 * rows, HEAD_DIM)

    def attended(query_pair, key_pair, lanes):
        scores = lax.dot_general(
            both(query_pair, 0, lanes), both(key_pair, first, lanes), (((1,), (1,)), ((), ())),
            preferred_element_type=jnp.float32,
        )
        column = key_col[at_rows(query_pair, 2 * rows), :]
        line = key_line[0:1, at_rows(key_pair, 2 * rows)]
        causal = jnp.concatenate([column >= line[:, :rows], column >= line[:, rows:]], axis=1)
        weights = jnp.where(causal, scores, 0.0).astype(jnp.bfloat16)
        return jnp.dot(weights, both(key_pair, first + rows, lanes), preferred_element_type=jnp.float32)

    shares = [slice(start, start + HEAD_DIM) for start in range(0, width, HEAD_DIM)]

    def wait_pair(distance):
        across(1, 2 * distance + 1, False).wait_recv()

        @pl.when(distance > 0)
        def _():
            across(1, 2 * distance, False).wait_recv()

    def take_keys(distance):
        key_pair = partner(lax.div(me, 2), distance, pairs)
        for lanes in shares:
            for query_pair in range(pairs):
                total[query_pair * 2 * rows:(query_pair + 1) * 2 * rows, lanes] += attended(
                    query_pair, key_pair, lanes
                )

    def take_near(distance, _):
        wait_pair(distance)
        take_keys(distance)
        return 0

    def take_far(step, _):
        wait_pair(pairs - 1 - step)

        @pl.when(step < far - window)
        def _():
            send_pair(pairs - 1 - step - window)

        take_keys(pairs - 1 - step)
        return 0

    lax.fori_loop(0, near, take_near, 0)
    lax.fori_loop(0, far - 1, take_far, 0)
    wait_pair(near + me * 0)
    last_pair = partner(lax.div(me, 2), near, pairs)

    def finish(step, _):
        distance = pairs - 1 - step
        query_pair = partner(lax.div(me, 2), distance, pairs)
        at = at_rows(query_pair, 2 * rows)
        for lanes in shares:
            combined = total[at, lanes] + attended(query_pair, last_pair, lanes)
            scale = lax.rsqrt(jnp.mean(combined * combined, axis=-1, keepdims=True) + 1e-06)
            result[at, lanes] = (combined * scale).astype(jnp.bfloat16)
        across(2, 2 * distance + 1, True).start()

        @pl.when(distance > 0)
        def _():
            across(2, 2 * distance, True).start()

        return 0

    lax.fori_loop(0, pairs, finish, 0)

    def scaled(source, place):
        for start in range(0, width, HEAD_DIM):
            at = pl.ds(pl.multiple_of(place * width + start, HEAD_DIM), HEAD_DIM)
            gain = jnp.where(
                mode_col[...] == 0.0, gains[0:1, at],
                jnp.where(mode_col[...] == 1.0, gains[1:2, at], gains[2:3, at]),
            )
            normed = source[:, start:start + HEAD_DIM].astype(jnp.float32)
            out_ref[:, at] = (normed * gain).astype(out_ref.dtype)

    scaled(result.at[at_rows(me, rows)], me)

    def settle(step, _):
        distance = step + 1
        for kind in range(4):
            across(kind, distance, True).wait_send()
        across(2, distance, False).wait_recv()
        other = partner(me, distance, count)
        scaled(back.at[other], other)
        return 0

    lax.fori_loop(0, count - 1, settle, 0)


def attend_by_heads(q_rows, k_rows, v_rows, block_of, modality, out_gain):
    rows, row_width = q_rows.shape
    count = lax.axis_size("seq")
    tokens = rows * count
    width = row_width // count
    anywhere = pl.BlockSpec(memory_space=pl.ANY)
    message = pltpu.VMEM((count, 3 * rows, width), q_rows.dtype)
    return pl.pallas_call(
        functools.partial(heads_kernel, count),
        out_shape=jax.ShapeDtypeStruct((rows, row_width), q_rows.dtype),
        in_specs=[anywhere] * 6,
        out_specs=pl.BlockSpec(memory_space=pltpu.VMEM),
        scratch_shapes=[
            pltpu.VMEM((3, rows, row_width), q_rows.dtype),
            pltpu.VMEM((1, rows), jnp.int32),
            pltpu.VMEM((1, rows), jnp.int32),
            pltpu.VMEM(out_gain.shape, jnp.float32),
            message,
            message,
            pltpu.VMEM((count, 1, rows), jnp.int32),
            pltpu.VMEM((8, tokens), jnp.float32),
            pltpu.VMEM((tokens, rows), jnp.float32),
            pltpu.VMEM((rows, rows), jnp.float32),
            pltpu.VMEM((tokens, width), jnp.float32),
            pltpu.VMEM((tokens, width), q_rows.dtype),
            pltpu.VMEM((count, rows, width), q_rows.dtype),
            pltpu.SemaphoreType.DMA((4, count)),
            pltpu.SemaphoreType.DMA((4, count)),
            pltpu.SemaphoreType.DMA((6,)),
        ],
        compiler_params=pltpu.CompilerParams(
            collective_id=0, has_side_effects=True, vmem_limit_bytes=56 * 2**20
        ),
        cost_estimate=pl.CostEstimate(
            flops=4 * tokens * tokens * width, bytes_accessed=8 * rows * row_width, transcendentals=tokens
        ),
    )(q_rows, k_rows, v_rows, block_of.reshape(1, rows), modality.reshape(1, rows), out_gain)


def entering(part, axis):
    place = lax.axis_index(axis)
    count = lax.axis_size(axis)
    state = lax.ppermute(part, axis, [(i, i + 1) for i in range(count - 1)])
    reach = 1
    while reach < count:
        state = state + lax.ppermute(state, axis, [(i, i + reach) for i in range(count - reach)])
        reach *= 2
    return state


def block_state(key_rows, value_rows):
    return jnp.einsum("shd,she->hde", key_rows, value_rows, preferred_element_type=jnp.float32)


def attend(queries, row_order, key_rows, value_rows, carried):
    row_count = queries.shape[0]
    head_count = queries.shape[1]
    slot_count = key_rows.shape[0]
    group_size = math.gcd(head_count, 4)
    carried_part = jnp.einsum("rhd,hde->rhe", queries, carried, preferred_element_type=jnp.float32)
    causal = row_order[:, None] >= jnp.arange(slot_count, dtype=jnp.int32)[None, :]

    def one_group(group_id):
        query_group = lax.dynamic_slice_in_dim(queries, group_id * group_size, group_size, 1)
        key_group = lax.dynamic_slice_in_dim(key_rows, group_id * group_size, group_size, 1)
        value_group = lax.dynamic_slice_in_dim(value_rows, group_id * group_size, group_size, 1)
        scores = jnp.einsum(
            "rhd,shd->hrs", query_group, key_group, preferred_element_type=jnp.float32
        )
        weights = jnp.where(causal[None], scores, 0.0).astype(jnp.bfloat16)
        return jnp.einsum("hrs,she->rhe", weights, value_group, preferred_element_type=jnp.float32)

    pieces = lax.map(one_group, jnp.arange(head_count // group_size, dtype=jnp.int32))
    local_part = jnp.moveaxis(pieces, 0, 1).reshape(row_count, head_count, queries.shape[2])
    combined = carried_part + local_part
    scale = lax.rsqrt(jnp.mean(combined * combined, axis=-1, keepdims=True) + 1e-06)
    return (combined * scale).astype(jnp.bfloat16)


def attend_by_blocks(q_rows, k_rows, v_rows, block_of, modality, out_gain):
    tok_count = q_rows.shape[0]
    row_width = q_rows.shape[1]
    peer_count = lax.axis_size("seq")
    capacity = max(2, 3 * tok_count // (2 * peer_count))
    slot_count = peer_count * capacity
    target = block_of[:, 0]
    place = jnp.arange(tok_count, dtype=jnp.int32)
    earlier_same = (target[:, None] == target[None, :]) & (place[None, :] < place[:, None])
    slot_rank = jnp.sum(earlier_same.astype(jnp.int32), axis=1)
    slot_index = target * capacity + slot_rank

    def routed(row_block):
        buffer = jnp.zeros((slot_count, row_width), row_block.dtype).at[slot_index].set(row_block)
        moved = lax.all_to_all(
            buffer.reshape(peer_count, capacity, row_width), "seq", split_axis=0, concat_axis=0, tiled=True
        )
        return moved.reshape(slot_count, HEADS, HEAD_DIM)

    queries, key_rows, value_rows = routed(q_rows), routed(k_rows), routed(v_rows)
    prefix = entering(block_state(key_rows, value_rows), "seq")
    carried = prefix.astype(jnp.bfloat16)
    normed = attend(queries, jnp.arange(slot_count, dtype=jnp.int32), key_rows, value_rows, carried)
    returned = lax.all_to_all(
        normed.reshape(peer_count, capacity, row_width), "seq", split_axis=0, concat_axis=0, tiled=True
    )
    own_rows = returned.reshape(slot_count, row_width)[slot_index]
    chosen = modality[:, None]
    gains = jnp.where(
        chosen == 0,
        out_gain[0][None, :],
        jnp.where(chosen == 1, out_gain[1][None, :], out_gain[2][None, :]),
    )
    return (own_rows.astype(jnp.float32) * gains).astype(jnp.bfloat16)


def on_device(q_rows, k_rows, v_rows, block_of, modality, out_gain):
    rows = q_rows.shape[0]
    count = lax.axis_size("seq")
    by_heads = count > 1 and HEADS % count == 0 and rows == HEAD_DIM
    plan = attend_by_heads if by_heads else attend_by_blocks
    return plan(q_rows, k_rows, v_rows, block_of, modality, out_gain)


def solution(mesh):
    placed = (
        P(("groups", "seq"), None),
        P(("groups", "seq"), None),
        P(("groups", "seq"), None),
        P(("groups", "seq"), None),
        P(("groups", "seq")),
        P(),
    )
    return jax.shard_map(
        on_device, mesh=mesh, in_specs=placed, out_specs=P(("groups", "seq"), None), check_vma=False
    )
```
